256 devices in a mesh: cand: 64 (over y, z, x_lo), param: 4 (over x_hi, core).
Axes of the slice: x: 4 (x_hi: 2, x_lo: 2; x = x_hi * 2 + x_lo), y: 4, z: 8, core: 2. Of those that a mesh axis runs over, the one named last changes fastest.
Arguments:
- candidate_rows: bfloat16 [32768, 8192], P('cand', 'param'), may hold values from -6 to 6
- sigma_rows: bfloat16 [32768, 8192], P('cand', 'param'), may hold values from -0.0625 to 0.0625
- sigma_sq_rows: bfloat16 [32768, 8192], P('cand', 'param'), may hold values from -0.0625 to 0.0625
- direction: bfloat16 [32768], P('cand'), may hold values from -0.119628906 to 0.119628906
- relaxed: float32 [32768], P(('cand', 'param')), may hold values from 0.05 to 0.95
Outputs:
- newton_residual: float32 [32768], P(('cand', 'param'))
The draws below stay inside these ranges and needn't reach their ends.
All inputs are finite; a program needn't handle non-finite values.
Results may differ from the reference program's by a relative error of at most 0.0003.
Values may be sent and summed in bfloat16 or wider, within the bound.
A program may use at most 64 MiB of HBM per device.

```python
import jax
import jax.numpy as jnp
from jax import lax

PARAM_COUNT = 8192
BLOCK_CANDIDATES = 512
PARTNERS = 2
CANDS = 32768
N_CAND = 64


def block_scale(own_key, extent, split, smallest, high):
    factor_of, own = 1.0, jax.random.fold_in(own_key, 6)
    for dim, blocks in split:
        steps = jnp.exp(jax.random.uniform(jax.random.fold_in(own, dim), (blocks,), jnp.float32, smallest / len(split), high / len(split)))
        factor_of = factor_of * jnp.repeat(steps, extent[dim] // blocks).reshape([-1 if axis == dim else 1 for axis in range(len(extent))])
    return factor_of


def bell_draw(key, extent, scale, bound, split=(), kind=jnp.bfloat16):
    entries = scale * jax.random.normal(key, extent, jnp.float32)
    if split:
        entries = entries * block_scale(key, extent, split, -0.22, 0.18)
    return jnp.clip(entries, -bound, bound).astype(kind)


def setup_inputs(seed: int = 0) -> dict:
    keys = jax.random.split(jax.random.key(seed), 6)
    return {
        "candidate_rows": bell_draw(keys[0], (CANDS, PARAM_COUNT), 1.0, 6.0, ((0, 64), (1, 4))),
        "sigma_rows": bell_draw(keys[1], (CANDS, PARAM_COUNT), PARAM_COUNT ** -0.5, 0.0625, ((0, 64), (1, 4))),
        "sigma_sq_rows": bell_draw(keys[2], (CANDS, PARAM_COUNT), PARAM_COUNT ** -0.5, 0.0625, ((0, 64), (1, 4))),
        "direction": bell_draw(keys[3], (CANDS,), 0.02, 0.119628906, ((0, 64),)),
        "relaxed": jnp.clip(0.05 + 0.9 * jax.random.uniform(keys[4], (CANDS,), jnp.float32) ** block_scale(keys[4], (CANDS,), ((0, 256),), -0.2, 0.2), 0.05, 0.95),
    }


barrier_weight = 0.1


def build_gram_tile(left_one, left_two, right_one, right_two):
    first = jnp.dot(left_one.astype(jnp.float32), right_one.astype(jnp.float32).T, precision=lax.Precision.HIGHEST)
    second = jnp.dot(left_two.astype(jnp.float32), right_two.astype(jnp.float32).T, precision=lax.Precision.HIGHEST)
    return 2.0 * first * second


def reference(candidate_rows, sigma_rows, sigma_sq_rows, direction, relaxed):
    measurement_rows = candidate_rows.reshape(N_CAND, BLOCK_CANDIDATES, PARAM_COUNT)
    sig = sigma_rows.reshape(N_CAND, BLOCK_CANDIDATES, PARAM_COUNT)
    sigsq = sigma_sq_rows.reshape(N_CAND, BLOCK_CANDIDATES, PARAM_COUNT)
    vector_rows = direction.astype(jnp.float32).reshape(N_CAND, BLOCK_CANDIDATES)

    def one_block(block_index):
        local_vectors = measurement_rows[block_index]
        local_slack = sig[block_index]
        local_quadratic = sigsq[block_index]
        residual_output = jnp.dot(build_gram_tile(local_vectors, local_vectors, local_slack, local_quadratic), vector_rows[block_index], precision=lax.Precision.HIGHEST)
        for step in range(1, PARTNERS + 1):
            before = (block_index - step) % N_CAND
            later_block = (block_index + step) % N_CAND
            residual_output = residual_output + jnp.dot(build_gram_tile(local_vectors, local_vectors, sig[before], sigsq[before]), vector_rows[before], precision=lax.Precision.HIGHEST)
            residual_output = residual_output + jnp.dot(build_gram_tile(local_slack, local_quadratic, measurement_rows[later_block], measurement_rows[later_block]), vector_rows[later_block], precision=lax.Precision.HIGHEST)
        diag_terms = jnp.sum(local_vectors.astype(jnp.float32) * local_quadratic.astype(jnp.float32), axis=1)
        return residual_output, diag_terms

    products, diag_all = lax.map(one_block, jnp.arange(N_CAND, dtype=jnp.int32))
    products = products.reshape(CANDS)
    diag_all = diag_all.reshape(CANDS)
    zval = relaxed
    grad = -diag_all - barrier_weight * (1.0 / zval - 1.0 / (1.0 - zval))
    curve = barrier_weight * (1.0 / (zval * zval) + 1.0 / ((1.0 - zval) * (1.0 - zval)))
    return products + grad + curve * direction.astype(jnp.float32)
```

```python
import jax
import jax.numpy as jnp
from jax import lax
from jax.experimental import pallas as pl
from jax.experimental.pallas import tpu as pltpu
from jax.sharding import PartitionSpec as P

PARTNERS = 2
barrier_weight = 0.1

MESH = pl.DeviceIdType.MESH
ROWS = 128
CHUNKS = 4
STEPS = 3 * CHUNKS
HALF = 256
LAST = (((1,), (1,)), ((), ()))
FIRST = (((1,), (0,)), ((), ()))


def exact_dot(left, right, dims):
    return lax.dot_general(
        left, right, dims, precision=lax.Precision.HIGHEST, preferred_element_type=jnp.float32
    )


def kernel(
    a_in, s_in, q_in, v_in, out,
    rows, sq, vec, g_send, g_recv, g_own, k_send, k_recv, col, m_send, m_recv,
    load_sem, z_send_sem, z_recv_sem, x_send_sem, x_recv_sem, g_send_sem, g_recv_sem,
    k_send_sem, k_recv_sem, m_send_sem, m_recv_sem, v_send_sem, v_recv_sem,
):
    cand, param = lax.axis_index("cand"), lax.axis_index("param")
    blocks = lax.axis_size("cand")
    odd, core, x_hi = lax.rem(cand, 2), lax.rem(param, 2), param // 2

    def block_at(by):
        return lax.rem(cand + blocks + by, blocks)

    loads = []
    for chunk in range(CHUNKS):
        loads.append((a_in.at[pl.ds(chunk * ROWS, ROWS)], rows.at[0, chunk]))
    for half in range(2):
        part = pl.ds(half * HALF, HALF)
        loads.append((s_in.at[part], sq.at[half, pl.ds(0, HALF)]))
        loads.append((q_in.at[part], sq.at[half, pl.ds(HALF, HALF)]))
    loads = [
        pltpu.make_async_copy(source, target, load_sem.at[i])
        for i, (source, target) in enumerate(loads)
    ]
    for load in loads:
        load.start()

    barrier = pltpu.get_barrier_semaphore()
    partners = 0
    for by in (-2, -1, 0, 1, 2):
        for turn in range(4):
            if by == 0 and turn == 0:
                continue
            pl.semaphore_signal(
                barrier, inc=1, device_id=(block_at(by), lax.rem(param + turn, 4)),
                device_id_type=MESH,
            )
            partners += 1
    pl.semaphore_wait(barrier, partners)

    def to_two_before(chunk):
        return pltpu.make_async_remote_copy(
            src_ref=a_in.at[pl.ds(chunk * ROWS, ROWS)], dst_ref=rows.at[2, chunk],
            send_sem=z_send_sem.at[chunk], recv_sem=z_recv_sem.at[chunk],
            device_id=(block_at(-2), param), device_id_type=MESH,
        )

    def to_pair(chunk, source):
        return pltpu.make_async_remote_copy(
            src_ref=source, dst_ref=rows.at[1, chunk],
            send_sem=x_send_sem.at[chunk], recv_sem=x_recv_sem.at[chunk],
            device_id=(cand + 1 - 2 * odd, param), device_id_type=MESH,
        )

    def vec_to(by):
        return pltpu.make_async_remote_copy(
            src_ref=v_in, dst_ref=vec.at[by - 1],
            send_sem=v_send_sem.at[by - 1], recv_sem=v_recv_sem.at[by - 1],
            device_id=(block_at(-by), param), device_id_type=MESH,
        )

    for chunk in range(CHUNKS):
        to_two_before(chunk).start()

        @pl.when(odd == 1)
        def _():
            to_pair(chunk, a_in.at[pl.ds(chunk * ROWS, ROWS)]).start()

    for by in (1, 2):
        vec_to(by).start()

    col[...] = jnp.zeros_like(col)
    for load in loads:
        load.wait()

    def place(step):
        late = step - CHUNKS
        own = step < CHUNKS
        chunk = jnp.where(own, step, late // 2)
        by = jnp.where(own, 0, 2 - lax.rem(late + 2 * CHUNKS, 2))
        return by, chunk

    def to_core(step):
        return pltpu.make_async_remote_copy(
            src_ref=g_send.at[step], dst_ref=g_recv.at[step],
            send_sem=g_send_sem.at[step], recv_sem=g_recv_sem.at[step],
            device_id=(cand, param + 1 - 2 * core), device_id_type=MESH,
        )

    def to_chip(step):
        return pltpu.make_async_remote_copy(
            src_ref=k_send.at[step], dst_ref=k_recv.at[step],
            send_sem=k_send_sem.at[step], recv_sem=k_recv_sem.at[step],
            device_id=(cand, lax.rem(param + 2, 4)), device_id_type=MESH,
        )

    def message(index, slot, by, target):
        return pltpu.make_async_remote_copy(
            src_ref=m_send.at[index], dst_ref=m_recv.at[slot],
            send_sem=m_send_sem.at[index], recv_sem=m_recv_sem.at[slot],
            device_id=(block_at(by), target), device_id_type=MESH,
        )

    def products(step):
        by, chunk = place(step)

        @pl.when(by == 1)
        def _():
            to_pair(chunk, rows.at[2, chunk]).wait_recv()

        @pl.when(by == 2)
        def _():
            to_two_before(chunk).wait_recv()

            @pl.when(odd == 0)
            def _():
                to_pair(chunk, rows.at[2, chunk]).start()

        g_send[step] = lax.dot_general(
            rows[by, chunk], sq[1 - core], LAST, preferred_element_type=jnp.float32
        )
        to_core(step).start()
        g_own[step] = lax.dot_general(
            rows[by, chunk], sq[core], LAST, preferred_element_type=jnp.float32
        )

    def between_cores(step):
        to_core(step).wait_recv()
        total = g_own[step] + g_recv[step]
        g_own[step] = total
        k_send[step] = total[:, HALF:]
        to_chip(step).start()

    def between_chips(step):
        by, chunk = place(step)
        to_chip(step).wait_recv()
        total = g_own[step]
        tile = total[:, :HALF] * (total[:, HALF:] + k_recv[step])
        own_vec = 2.0 * jnp.concatenate([v_in[2 * core], v_in[2 * core + 1]], axis=1)
        m_send[step] = exact_dot(own_vec, tile, LAST)

        @pl.when(by > 0)
        def _():
            col[...] += exact_dot(2.0 * vec[by - 1, chunk], tile, FIRST)

        @pl.when(jnp.logical_and(by == 0, chunk // 2 == core))
        def _():
            square = jnp.where(
                lax.rem(chunk, 2) == 0, total[:, HALF : HALF + ROWS], total[:, HALF + ROWS :]
            )
            line = lax.broadcasted_iota(jnp.int32, (ROWS, ROWS), 0)
            place_in = lax.broadcasted_iota(jnp.int32, (ROWS, ROWS), 1)
            square = jnp.where(line == place_in, square, 0.0)
            m_send[step] -= jnp.broadcast_to(jnp.sum(square, axis=0, keepdims=True), (8, ROWS))

        stays = jnp.logical_and(by == 0, chunk == param)

        @pl.when(stays)
        def _():
            m_recv[param] = m_send[step]

        @pl.when(jnp.logical_not(stays))
        def _():
            message(step, by * 4 + param, by, chunk).start()

    def one(step, carry):
        @pl.when(jnp.logical_and(step >= 1, step <= STEPS))
        def _():
            between_cores(step - 1)

        @pl.when(step < STEPS)
        def _():
            products(step)

        @pl.when(step >= LAG)
        def _():
            between_chips(step - LAG)

        return carry

    LAG = 3
    lax.fori_loop(0, CHUNKS, one, 0)
    for by in (1, 2):
        vec_to(by).wait()
    lax.fori_loop(CHUNKS, STEPS + LAG, one, 0)

    for part in range(2):
        m_send[STEPS + part] = col[:, part * ROWS : (part + 1) * ROWS]
        target = 2 * core + part

        @pl.when(target == param)
        def _():
            m_recv[12 + x_hi] = m_send[STEPS + part]

        @pl.when(target != param)
        def _():
            message(STEPS + part, 12 + x_hi, 0, target).start()

    for source in range(4):
        @pl.when(source != param)
        def _():
            message(0, source, 0, param).wait_recv()

        message(0, 4 + source, 1, param).wait_recv()
        message(0, 8 + source, 2, param).wait_recv()
    for high in range(2):
        @pl.when(2 * high + param // 2 != param)
        def _():
            message(0, 12 + high, 0, param).wait_recv()

    out[...] = jnp.sum(m_recv[...], axis=0)

    def drain(step, carry):
        to_core(step).wait_send()
        to_chip(step).wait_send()
        by, chunk = place(step)

        @pl.when(jnp.logical_not(jnp.logical_and(by == 0, chunk == param)))
        def _():
            message(step, 0, by, chunk).wait_send()

        return carry

    lax.fori_loop(0, STEPS, drain, 0)
    for part in range(2):
        @pl.when(2 * core + part != param)
        def _():
            message(STEPS + part, 0, 0, param).wait_send()

    for chunk in range(CHUNKS):
        to_two_before(chunk).wait_send()
        to_pair(chunk, rows.at[2, chunk]).wait_send()


def hessian_product(candidate_rows, sigma_rows, sigma_sq_rows, vectors):
    width, depth = candidate_rows.shape
    f32 = jnp.float32
    dma = pltpu.SemaphoreType.DMA
    return pl.pallas_call(
        kernel,
        out_shape=jax.ShapeDtypeStruct((8, ROWS), f32),
        in_specs=[pl.BlockSpec(memory_space=pl.ANY)] * 3 + [pl.BlockSpec(memory_space=pltpu.VMEM)],
        out_specs=pl.BlockSpec(memory_space=pltpu.VMEM),
        scratch_shapes=[
            pltpu.VMEM((3, CHUNKS, ROWS, depth), jnp.bfloat16),
            pltpu.VMEM((2, width, depth), jnp.bfloat16),
            pltpu.VMEM((2, CHUNKS, 8, ROWS), f32),
            pltpu.VMEM((STEPS, ROWS, width), f32),
            pltpu.VMEM((STEPS, ROWS, width), f32),
            pltpu.VMEM((STEPS, ROWS, width), f32),
            pltpu.VMEM((STEPS, ROWS, HALF), f32),
            pltpu.VMEM((STEPS, ROWS, HALF), f32),
            pltpu.VMEM((8, HALF), f32),
            pltpu.VMEM((STEPS + 2, 8, ROWS), f32),
            pltpu.VMEM((14, 8, ROWS), f32),
            dma((CHUNKS + 4,)),
            dma((CHUNKS,)), dma((CHUNKS,)), dma((CHUNKS,)), dma((CHUNKS,)),
            dma((STEPS,)), dma((STEPS,)), dma((STEPS,)), dma((STEPS,)),
            dma((STEPS + 2,)), dma((14,)), dma((2,)), dma((2,)),
        ],
        compiler_params=pltpu.CompilerParams(
            collective_id=1, has_side_effects=True, vmem_limit_bytes=40 * 2**20
        ),
        name="hessian_product",
    )(candidate_rows, sigma_rows, sigma_sq_rows, vectors)


def body(candidate_rows, sigma_rows, sigma_sq_rows, direction, relaxed):
    width = candidate_rows.shape[0]
    share = width // lax.axis_size("param")
    first_row = lax.axis_index("param") * share
    own_vec = direction.astype(jnp.float32)
    own_slice = lax.dynamic_slice_in_dim(own_vec, first_row, share, 0)
    vectors = jnp.broadcast_to(own_vec.reshape(CHUNKS, 1, ROWS), (CHUNKS, 8, ROWS))
    product = hessian_product(candidate_rows, sigma_rows, sigma_sq_rows, vectors)[0]
    slope = barrier_weight * (1.0 / relaxed - 1.0 / (1.0 - relaxed))
    curve = barrier_weight * (1.0 / (relaxed * relaxed) + 1.0 / ((1.0 - relaxed) * (1.0 - relaxed)))
    return product - slope + curve * own_slice


def solution(mesh):
    return jax.shard_map(
        body,
        mesh=mesh,
        in_specs=(
            P("cand", "param"),
            P("cand", "param"),
            P("cand", "param"),
            P("cand"),
            P(("cand", "param")),
        ),
        out_specs=P(("cand", "param")),
        check_vma=False,
    )
```

```python
import jax
import jax.numpy as jnp
from jax import lax
from jax.experimental import pallas as pl
from jax.experimental.pallas import tpu as pltpu
from jax.sharding import PartitionSpec as P

PARTNERS = 2
barrier_weight = 0.1

MESH = pl.DeviceIdType.MESH
ROWS = 64
CHUNKS = 8
STEPS = 3 * CHUNKS
HALF = 256
SHARE = 128
SPAN = 256
AHEAD = 2
LAG = 4
REACH = 125.0
LAST = (((1,), (1,)), ((), ()))
FIRST = (((1,), (0,)), ((), ()))


def exact_dot(left, right, dims):
    return lax.dot_general(
        left, right, dims, precision=lax.Precision.HIGHEST, preferred_element_type=jnp.float32
    )


def kernel(
    a_in, s_in, q_in, v_in, out,
    rows, sq, sqt, vec, g_send, g_recv, g_own, k_send, k_recv, col, line, m_send, m_recv,
    load_sem, z_send_sem, z_recv_sem, x_send_sem, x_recv_sem, g_send_sem, g_recv_sem,
    k_send_sem, k_recv_sem, m_send_sem, m_recv_sem, v_send_sem, v_recv_sem,
):
    cand, param = lax.axis_index("cand"), lax.axis_index("param")
    blocks = lax.axis_size("cand")
    odd, core, x_hi = lax.rem(cand, 2), lax.rem(param, 2), param // 2

    def block_at(by):
        return lax.rem(cand + blocks + by, blocks)

    loads = []
    for chunk in range(CHUNKS):
        loads.append((a_in.at[pl.ds(chunk * ROWS, ROWS)], rows.at[0, chunk]))
    for half in range(2):
        part = pl.ds(half * HALF, HALF)
        loads.append((s_in.at[part], sq.at[half, pl.ds(0, HALF)]))
        loads.append((q_in.at[part], sq.at[half, pl.ds(HALF, HALF)]))
    loads = [
        pltpu.make_async_copy(source, target, load_sem.at[i])
        for i, (source, target) in enumerate(loads)
    ]
    for load in loads:
        load.start()

    barrier = pltpu.get_barrier_semaphore()
    partners = 0
    for by in (-2, -1, 0, 1, 2):
        for turn in range(4):
            if by == 0 and turn == 0:
                continue
            pl.semaphore_signal(
                barrier, inc=1, device_id=(block_at(by), lax.rem(param + turn, 4)),
                device_id_type=MESH,
            )
            partners += 1
    pl.semaphore_wait(barrier, partners)

    def own_rows(chunk):
        return a_in.at[pl.ds(pl.multiple_of(chunk * ROWS, ROWS), ROWS)]

    def to_two_before(chunk):
        return pltpu.make_async_remote_copy(
            src_ref=own_rows(chunk), dst_ref=rows.at[2, chunk],
            send_sem=z_send_sem.at[chunk], recv_sem=z_recv_sem.at[chunk],
            device_id=(block_at(-2), param), device_id_type=MESH,
        )

    def to_pair(chunk, source):
        return pltpu.make_async_remote_copy(
            src_ref=source, dst_ref=rows.at[1, chunk],
            send_sem=x_send_sem.at[chunk], recv_sem=x_recv_sem.at[chunk],
            device_id=(cand + 1 - 2 * odd, param), device_id_type=MESH,
        )

    def vec_to(by):
        return pltpu.make_async_remote_copy(
            src_ref=v_in, dst_ref=vec.at[by - 1],
            send_sem=v_send_sem.at[by - 1], recv_sem=v_recv_sem.at[by - 1],
            device_id=(block_at(-by), param), device_id_type=MESH,
        )

    def send_own(chunk):
        to_two_before(chunk).start()

        @pl.when(odd == 1)
        def _():
            to_pair(chunk, own_rows(chunk)).start()

    send_own(0)
    for by in (1, 2):
        vec_to(by).start()

    col[...] = jnp.zeros_like(col)
    for load in loads[CHUNKS:]:
        load.wait()

    def turn(piece, carry):
        at = pl.ds(pl.multiple_of(piece * SPAN, SPAN), SPAN)
        for half in range(2):
            sqt[half, at, :] = sq[half, :, at].T
        return carry

    lax.fori_loop(0, sq.shape[2] // SPAN, turn, 0)
    for load in loads[:CHUNKS]:
        load.wait()

    def place(step):
        late = jnp.maximum(step - CHUNKS, 0)
        far = jnp.logical_or(late == 0, jnp.logical_and(lax.rem(late, 2) == 1, late < 2 * CHUNKS - 1))
        by = jnp.where(step < CHUNKS, 0, jnp.where(far, 2, 1))
        chunk = jnp.where(far, (late + 1) // 2, jnp.maximum(late - 1, 0) // 2)
        return by, jnp.where(step < CHUNKS, step, chunk)

    def to_core(step):
        return pltpu.make_async_remote_copy(
            src_ref=g_send.at[step], dst_ref=g_recv.at[step],
            send_sem=g_send_sem.at[step], recv_sem=g_recv_sem.at[step],
            device_id=(cand, param + 1 - 2 * core), device_id_type=MESH,
        )

    def to_chip(step):
        return pltpu.make_async_remote_copy(
            src_ref=k_send.at[step], dst_ref=k_recv.at[step],
            send_sem=k_send_sem.at[step], recv_sem=k_recv_sem.at[step],
            device_id=(cand, lax.rem(param + 2, 4)), device_id_type=MESH,
        )

    def message(index, slot, by, target):
        return pltpu.make_async_remote_copy(
            src_ref=m_send.at[index], dst_ref=m_recv.at[slot],
            send_sem=m_send_sem.at[index], recv_sem=m_recv_sem.at[slot],
            device_id=(block_at(by), target), device_id_type=MESH,
        )

    def products(step):
        by, chunk = place(step)

        @pl.when(by == 1)
        def _():
            to_pair(chunk, rows.at[2, chunk]).wait_recv()

        @pl.when(by == 2)
        def _():
            to_two_before(chunk).wait_recv()

            @pl.when(odd == 0)
            def _():
                to_pair(chunk, rows.at[2, chunk]).start()

            @pl.when(chunk + AHEAD < CHUNKS)
            def _():
                send_own(chunk + AHEAD)

        for early in range(1, AHEAD):
            @pl.when(step == 3 * early)
            def _():
                send_own(early)

        g_send[step] = lax.dot_general(
            rows[by, chunk], sqt[1 - core], FIRST, preferred_element_type=jnp.float32
        )
        to_core(step).start()
        g_own[step] = lax.dot_general(
            rows[by, chunk], sqt[core], FIRST, preferred_element_type=jnp.float32
        )

    def coded(values):
        scale = jnp.max(jnp.abs(values), axis=0, keepdims=True) * 1.01 + 1e-30
        scale = scale.astype(jnp.bfloat16).astype(jnp.float32)
        power = jnp.exp2(jnp.abs(values) * (2.0 * REACH / scale) - REACH)
        return jnp.where(values < 0.0, -power, power), scale

    def decoded(code, scale):
        size = (jnp.log2(jnp.abs(code)) + REACH) * (scale * (0.5 / REACH))
        return jnp.where(code < 0.0, -size, size)

    def between_cores(step):
        to_core(step).wait_recv()
        total = g_own[step] + g_recv[step]
        g_own[step] = total
        code, scale = coded(total[:, HALF:])
        k_send[step, :ROWS] = code.astype(jnp.bfloat16)
        k_send[step, ROWS:] = jnp.broadcast_to(scale, (16, HALF)).astype(jnp.bfloat16)
        to_chip(step).start()

    def between_chips(step):
        by, chunk = place(step)
        to_chip(step).wait_recv()
        total = g_own[step]
        other = decoded(
            k_recv[step, :ROWS].astype(jnp.float32),
            k_recv[step, ROWS:].astype(jnp.float32)[:1],
        )
        tile = total[:, :HALF] * (total[:, HALF:] + other)
        own_vec = 2.0 * jnp.concatenate([v_in[2 * core], v_in[2 * core + 1]], axis=1)
        line[by, lax.rem(chunk, 2)] = exact_dot(own_vec, tile, LAST)

        @pl.when(by > 0)
        def _():
            pair = vec[jnp.maximum(by - 1, 0), chunk // 2]
            part = jnp.where(lax.rem(chunk, 2) == 0, pair[:, :ROWS], pair[:, ROWS:])
            col[...] += exact_dot(2.0 * part, tile, FIRST)

        @pl.when(jnp.logical_and(by == 0, chunk // 4 == core))
        def _():
            down = lax.broadcasted_iota(jnp.int32, (ROWS, HALF), 0)
            across = lax.broadcasted_iota(jnp.int32, (ROWS, HALF), 1)
            square = jnp.where(down + lax.rem(chunk, 4) * ROWS == across, total[:, HALF:], 0.0)
            col[...] -= jnp.broadcast_to(jnp.sum(square, axis=0, keepdims=True), (8, HALF))

        target = chunk // 2
        index = by * 4 + target
        stays = jnp.logical_and(by == 0, target == param)
        whole = lax.rem(chunk, 2) == 1

        @pl.when(whole)
        def _():
            m_send[index] = jnp.concatenate([line[by, 0], line[by, 1]], axis=1)

        @pl.when(jnp.logical_and(whole, stays))
        def _():
            m_recv[param] = m_send[index]

        @pl.when(jnp.logical_and(whole, jnp.logical_not(stays)))
        def _():
            message(index, by * 4 + param, by, target).start()

    def one(step, carry):
        @pl.when(jnp.logical_and(step >= 1, step <= STEPS))
        def _():
            between_cores(step - 1)

        @pl.when(step >= LAG)
        def _():
            between_chips(step - LAG)

        @pl.when(step < STEPS)
        def _():
            products(step)

        return carry

    lax.fori_loop(0, CHUNKS, one, 0)
    for by in (1, 2):
        vec_to(by).wait()
    lax.fori_loop(CHUNKS, STEPS + LAG, one, 0)

    for part in range(2):
        m_send[12 + part] = col[:, part * SHARE : (part + 1) * SHARE]
        target = 2 * core + part

        @pl.when(target == param)
        def _():
            m_recv[12 + x_hi] = m_send[12 + part]

        @pl.when(target != param)
        def _():
            message(12 + part, 12 + x_hi, 0, target).start()

    for source in range(4):
        @pl.when(source != param)
        def _():
            message(0, source, 0, param).wait_recv()

        message(0, 4 + source, 1, param).wait_recv()
        message(0, 8 + source, 2, param).wait_recv()
    for high in range(2):
        @pl.when(2 * high + param // 2 != param)
        def _():
            message(0, 12 + high, 0, param).wait_recv()

    out[...] = jnp.sum(m_recv[...], axis=0)

    def drain(step, carry):
        to_core(step).wait_send()
        to_chip(step).wait_send()
        return carry

    lax.fori_loop(0, STEPS, drain, 0)
    for target in range(4):
        @pl.when(target != param)
        def _():
            message(target, 0, 0, target).wait_send()

        message(4 + target, 0, 1, target).wait_send()
        message(8 + target, 0, 2, target).wait_send()
    for part in range(2):
        @pl.when(2 * core + part != param)
        def _():
            message(12 + part, 0, 0, param).wait_send()

    for chunk in range(CHUNKS):
        to_two_before(chunk).wait_send()
        to_pair(chunk, rows.at[2, chunk]).wait_send()


def hessian_product(candidate_rows, sigma_rows, sigma_sq_rows, vectors):
    width, depth = candidate_rows.shape
    f32 = jnp.float32
    dma = pltpu.SemaphoreType.DMA
    return pl.pallas_call(
        kernel,
        out_shape=jax.ShapeDtypeStruct((8, SHARE), f32),
        in_specs=[pl.BlockSpec(memory_space=pl.ANY)] * 3 + [pl.BlockSpec(memory_space=pltpu.VMEM)],
        out_specs=pl.BlockSpec(memory_space=pltpu.VMEM),
        scratch_shapes=[
            pltpu.VMEM((3, CHUNKS, ROWS, depth), jnp.bfloat16),
            pltpu.VMEM((2, width, depth), jnp.bfloat16),
            pltpu.VMEM((2, depth, width), jnp.bfloat16),
            pltpu.VMEM((2, 4, 8, SHARE), f32),
            pltpu.VMEM((STEPS, ROWS, width), f32),
            pltpu.VMEM((STEPS, ROWS, width), f32),
            pltpu.VMEM((STEPS, ROWS, width), f32),
            pltpu.VMEM((STEPS, ROWS + 16, HALF), jnp.bfloat16),
            pltpu.VMEM((STEPS, ROWS + 16, HALF), jnp.bfloat16),
            pltpu.VMEM((8, HALF), f32),
            pltpu.VMEM((3, 2, 8, ROWS), f32),
            pltpu.VMEM((14, 8, SHARE), f32),
            pltpu.VMEM((14, 8, SHARE), f32),
            dma((CHUNKS + 4,)),
            dma((CHUNKS,)), dma((CHUNKS,)), dma((CHUNKS,)), dma((CHUNKS,)),
            dma((STEPS,)), dma((STEPS,)), dma((STEPS,)), dma((STEPS,)),
            dma((14,)), dma((14,)), dma((2,)), dma((2,)),
        ],
        compiler_params=pltpu.CompilerParams(
            collective_id=1, has_side_effects=True, vmem_limit_bytes=62 * 2**20
        ),
        name="hessian_product",
    )(candidate_rows, sigma_rows, sigma_sq_rows, vectors)


def body(candidate_rows, sigma_rows, sigma_sq_rows, direction, relaxed):
    width = candidate_rows.shape[0]
    share = width // lax.axis_size("param")
    first_row = lax.axis_index("param") * share
    own_vec = direction.astype(jnp.float32)
    own_slice = lax.dynamic_slice_in_dim(own_vec, first_row, share, 0)
    vectors = jnp.broadcast_to(own_vec.reshape(4, 1, SHARE), (4, 8, SHARE))
    product = hessian_product(candidate_rows, sigma_rows, sigma_sq_rows, vectors)[0]
    slope = barrier_weight * (1.0 / relaxed - 1.0 / (1.0 - relaxed))
    curve = barrier_weight * (1.0 / (relaxed * relaxed) + 1.0 / ((1.0 - relaxed) * (1.0 - relaxed)))
    return product - slope + curve * own_slice


def solution(mesh):
    return jax.shard_map(
        body,
        mesh=mesh,
        in_specs=(
            P("cand", "param"),
            P("cand", "param"),
            P("cand", "param"),
            P("cand"),
            P(("cand", "param")),
        ),
        out_specs=P(("cand", "param")),
        check_vma=False,
    )
```

```python
import jax
import jax.numpy as jnp
from jax import lax
from jax.experimental import pallas as pl
from jax.experimental.pallas import tpu as pltpu
from jax.sharding import PartitionSpec as P

PARTNERS = 2
barrier_weight = 0.1

MESH = pl.DeviceIdType.MESH
ROWS = 128
CHUNKS = 4
STEPS = 3 * CHUNKS
PIECE = 64
PIECES = 8
HALF = 256
SPAN = 256
AHEAD = 2
LAG = 4
REACH = 125.0
LAST = (((1,), (1,)), ((), ()))
FIRST = (((1,), (0,)), ((), ()))


def exact_dot(left, right, dims):
    return lax.dot_general(
        left, right, dims, precision=lax.Precision.HIGHEST, preferred_element_type=jnp.float32
    )


def coded(values):
    scale = jnp.max(jnp.abs(values), axis=0, keepdims=True) + 1e-30
    power = jnp.exp2(jnp.abs(values) * (2.0 * REACH / scale) - REACH)
    return jnp.where(values < 0.0, -power, power), scale


def decoded(code, scale):
    size = (jnp.log2(jnp.abs(code)) + REACH) * (scale * (0.5 / REACH))
    return jnp.where(code < 0.0, -size, size)


def kernel(
    a_in, s_in, q_in, v_in, z_in, out,
    rows, sq, sqt, own_vec, vec, g_send, g_recv, g_own, k_send, k_recv, w_send, w_recv, col, m_send, m_recv,
    load_sem, z_send_sem, z_recv_sem, x_send_sem, x_recv_sem, g_send_sem, g_recv_sem,
    k_send_sem, k_recv_sem, w_send_sem, w_recv_sem, m_send_sem, m_recv_sem, v_send_sem, v_recv_sem,
):
    cand, param = lax.axis_index("cand"), lax.axis_index("param")
    blocks = lax.axis_size("cand")
    odd, core, x_hi = lax.rem(cand, 2), lax.rem(param, 2), param // 2

    def block_at(by):
        return lax.rem(cand + blocks + by, blocks)

    loads = []
    for half in range(2):
        part = pl.ds(half * HALF, HALF)
        loads.append((s_in.at[part], sq.at[half, pl.ds(0, HALF)]))
        loads.append((q_in.at[part], sq.at[half, pl.ds(HALF, HALF)]))
    loads.append((a_in, rows.at[0]))
    loads = [
        pltpu.make_async_copy(source, target, load_sem.at[i])
        for i, (source, target) in enumerate(loads)
    ]
    for load in loads:
        load.start()

    barrier = pltpu.get_barrier_semaphore()
    partners = 0
    for by in (-2, -1, 0, 1, 2):
        for turn in range(4):
            if by == 0 and turn == 0:
                continue
            pl.semaphore_signal(
                barrier, inc=1, device_id=(block_at(by), lax.rem(param + turn, 4)),
                device_id_type=MESH,
            )
            partners += 1
    for part in range(4):
        own_vec[part] = jnp.broadcast_to(v_in[part : part + 1, :].astype(jnp.float32), (8, ROWS))
    col[...] = jnp.zeros_like(col)
    pl.semaphore_wait(barrier, partners)

    def own_piece(piece):
        return a_in.at[pl.ds(pl.multiple_of(piece * PIECE, PIECE), PIECE)]

    def landing(by, piece):
        return rows.at[by, pl.ds(pl.multiple_of(piece * PIECE, PIECE), PIECE)]

    def to_two_before(piece):
        return pltpu.make_async_remote_copy(
            src_ref=own_piece(piece), dst_ref=landing(2, piece),
            send_sem=z_send_sem.at[piece], recv_sem=z_recv_sem.at[piece],
            device_id=(block_at(-2), param), device_id_type=MESH,
        )

    def to_pair(piece, source):
        return pltpu.make_async_remote_copy(
            src_ref=source, dst_ref=landing(1, piece),
            send_sem=x_send_sem.at[piece], recv_sem=x_recv_sem.at[piece],
            device_id=(cand + 1 - 2 * odd, param), device_id_type=MESH,
        )

    def vec_to(by):
        return pltpu.make_async_remote_copy(
            src_ref=own_vec, dst_ref=vec.at[by - 1],
            send_sem=v_send_sem.at[by - 1], recv_sem=v_recv_sem.at[by - 1],
            device_id=(block_at(-by), param), device_id_type=MESH,
        )

    def send_own(piece):
        to_two_before(piece).start()

        @pl.when(odd == 1)
        def _():
            to_pair(piece, own_piece(piece)).start()

    def pass_on(piece):
        to_two_before(piece).wait_recv()

        @pl.when(odd == 0)
        def _():
            to_pair(piece, landing(2, piece)).start()

        @pl.when(piece + AHEAD < PIECES)
        def _():
            send_own(piece + AHEAD)

    send_own(0)
    for by in (1, 2):
        vec_to(by).start()

    for load in loads[:4]:
        load.wait()

    def turn(piece, carry):
        at = pl.ds(pl.multiple_of(piece * SPAN, SPAN), SPAN)
        for half in range(2):
            sqt[half, at, :] = sq[half, :, at].T
        return carry

    lax.fori_loop(0, sq.shape[2] // SPAN, turn, 0)
    loads[4].wait()

    def place(step):
        late = jnp.maximum(step - CHUNKS, 0)
        by = jnp.where(step < CHUNKS, 0, 2 - lax.rem(late, 2))
        return by, jnp.where(step < CHUNKS, step, late // 2)

    def to_core(step):
        return pltpu.make_async_remote_copy(
            src_ref=g_send.at[step], dst_ref=g_recv.at[step],
            send_sem=g_send_sem.at[step], recv_sem=g_recv_sem.at[step],
            device_id=(cand, param + 1 - 2 * core), device_id_type=MESH,
        )

    def to_chip(step):
        return pltpu.make_async_remote_copy(
            src_ref=k_send.at[step], dst_ref=k_recv.at[step],
            send_sem=k_send_sem.at[step], recv_sem=k_recv_sem.at[step],
            device_id=(cand, lax.rem(param + 2, 4)), device_id_type=MESH,
        )

    def scale_to_chip(step):
        return pltpu.make_async_remote_copy(
            src_ref=w_send.at[step], dst_ref=w_recv.at[step],
            send_sem=w_send_sem.at[step], recv_sem=w_recv_sem.at[step],
            device_id=(cand, lax.rem(param + 2, 4)), device_id_type=MESH,
        )

    def message(index, slot, by, target):
        return pltpu.make_async_remote_copy(
            src_ref=m_send.at[index], dst_ref=m_recv.at[slot],
            send_sem=m_send_sem.at[index], recv_sem=m_recv_sem.at[slot],
            device_id=(block_at(by), target), device_id_type=MESH,
        )

    def products(step):
        by, chunk = place(step)

        for early in range(1, AHEAD):
            @pl.when(step == early)
            def _():
                send_own(early)

        @pl.when(step == CHUNKS)
        def _():
            pass_on(0)

        @pl.when(jnp.logical_and(step >= CHUNKS, step < STEPS - 1))
        def _():
            pass_on(step - CHUNKS + 1)

        @pl.when(by == 1)
        def _():
            for part in range(2):
                to_pair(2 * chunk + part, landing(2, 2 * chunk + part)).wait_recv()

        left = rows[by, pl.ds(pl.multiple_of(chunk * ROWS, ROWS), ROWS), :]
        g_send[step] = lax.dot_general(
            left, sqt[1 - core], FIRST, preferred_element_type=jnp.float32
        )
        to_core(step).start()
        g_own[step] = lax.dot_general(
            left, sqt[core], FIRST, preferred_element_type=jnp.float32
        )

    def between_cores(step):
        to_core(step).wait_recv()
        total = g_own[step] + g_recv[step]
        g_own[step] = total
        code, scale = coded(total[:, HALF:])
        k_send[step] = code.astype(jnp.bfloat16)
        w_send[step] = scale
        to_chip(step).start()
        scale_to_chip(step).start()

    def between_chips(step):
        by, chunk = place(step)
        to_chip(step).wait_recv()
        total = g_own[step]
        scale_to_chip(step).wait_recv()
        other = decoded(k_recv[step].astype(jnp.float32), w_recv[step])
        tile = total[:, :HALF] * (total[:, HALF:] + other)
        half_vec = jnp.concatenate([own_vec[2 * core], own_vec[2 * core + 1]], axis=1)
        m_send[step] = exact_dot(2.0 * half_vec, tile, LAST)
        stays = jnp.logical_and(by == 0, chunk == param)

        @pl.when(stays)
        def _():
            m_recv[param] = m_send[step]

        @pl.when(jnp.logical_not(stays))
        def _():
            message(step, by * 4 + param, by, chunk).start()

        @pl.when(by > 0)
        def _():
            col[...] += exact_dot(2.0 * vec[jnp.maximum(by - 1, 0), chunk], tile, FIRST)

        @pl.when(jnp.logical_and(by == 0, chunk // 2 == core))
        def _():
            down = lax.broadcasted_iota(jnp.int32, (ROWS, HALF), 0)
            across = lax.broadcasted_iota(jnp.int32, (ROWS, HALF), 1)
            square = jnp.where(down + lax.rem(chunk, 2) * ROWS == across, total[:, HALF:], 0.0)
            col[...] -= jnp.broadcast_to(jnp.sum(square, axis=0, keepdims=True), (8, HALF))

    def first(step, carry):
        products(step)

        @pl.when(step >= 1)
        def _():
            between_cores(step - 1)

        return carry

    def later(step, carry):
        products(step)

        @pl.when(step >= LAG)
        def _():
            between_chips(step - LAG)

        between_cores(step)
        return carry

    def last(step, carry):
        between_chips(step)
        return carry

    lax.fori_loop(0, CHUNKS, first, 0)
    between_cores(CHUNKS - 1)
    for by in (1, 2):
        vec_to(by).wait()
    lax.fori_loop(CHUNKS, STEPS, later, 0)
    lax.fori_loop(STEPS - LAG, STEPS, last, 0)

    for part in range(2):
        m_send[STEPS + part] = col[:, part * ROWS : (part + 1) * ROWS]
        target = 2 * core + part

        @pl.when(target == param)
        def _():
            m_recv[12 + x_hi] = m_send[STEPS + part]

        @pl.when(target != param)
        def _():
            message(STEPS + part, 12 + x_hi, 0, target).start()

    zval = z_in[...]
    slope = barrier_weight * (1.0 / zval - 1.0 / (1.0 - zval))
    curve = barrier_weight * (1.0 / (zval * zval) + 1.0 / ((1.0 - zval) * (1.0 - zval)))
    own_terms = curve * own_vec[param][:1] - slope

    def drain(step, carry):
        to_core(step).wait_send()
        to_chip(step).wait_send()
        scale_to_chip(step).wait_send()
        by, chunk = place(step)

        @pl.when(jnp.logical_not(jnp.logical_and(by == 0, chunk == param)))
        def _():
            message(step, 0, by, chunk).wait_send()

        return carry

    lax.fori_loop(0, STEPS, drain, 0)
    for part in range(2):
        @pl.when(2 * core + part != param)
        def _():
            message(STEPS + part, 0, 0, param).wait_send()

    for piece in range(PIECES):
        to_two_before(piece).wait_send()
        to_pair(piece, landing(2, piece)).wait_send()

    for source in range(4):
        @pl.when(source != param)
        def _():
            message(0, source, 0, param).wait_recv()

        message(0, 4 + source, 1, param).wait_recv()
        message(0, 8 + source, 2, param).wait_recv()
    for high in range(2):
        @pl.when(2 * high + param // 2 != param)
        def _():
            message(0, 12 + high, 0, param).wait_recv()

    out[...] = jnp.sum(m_recv[...], axis=0)[:1] + own_terms


def body(candidate_rows, sigma_rows, sigma_sq_rows, direction, relaxed):
    width, depth = candidate_rows.shape
    f32, bf16 = jnp.float32, jnp.bfloat16
    dma = pltpu.SemaphoreType.DMA
    result = pl.pallas_call(
        kernel,
        out_shape=jax.ShapeDtypeStruct((1, ROWS), f32),
        in_specs=[pl.BlockSpec(memory_space=pl.ANY)] * 3
        + [pl.BlockSpec(memory_space=pltpu.VMEM)] * 2,
        out_specs=pl.BlockSpec(memory_space=pltpu.VMEM),
        scratch_shapes=[
            pltpu.VMEM((3, width, depth), bf16),
            pltpu.VMEM((2, width, depth), bf16),
            pltpu.VMEM((2, depth, width), bf16),
            pltpu.VMEM((4, 8, ROWS), f32),
            pltpu.VMEM((2, 4, 8, ROWS), f32),
            pltpu.VMEM((STEPS, ROWS, width), f32),
            pltpu.VMEM((STEPS, ROWS, width), f32),
            pltpu.VMEM((STEPS, ROWS, width), f32),
            pltpu.VMEM((STEPS, ROWS, HALF), bf16),
            pltpu.VMEM((STEPS, ROWS, HALF), bf16),
            pltpu.VMEM((STEPS, 1, HALF), f32),
            pltpu.VMEM((STEPS, 1, HALF), f32),
            pltpu.VMEM((8, HALF), f32),
            pltpu.VMEM((STEPS + 2, 8, ROWS), f32),
            pltpu.VMEM((14, 8, ROWS), f32),
            dma((5,)),
            dma((PIECES,)), dma((PIECES,)), dma((PIECES,)), dma((PIECES,)),
            dma((STEPS,)), dma((STEPS,)), dma((STEPS,)), dma((STEPS,)), dma((STEPS,)), dma((STEPS,)),
            dma((STEPS + 2,)), dma((14,)), dma((2,)), dma((2,)),
        ],
        compiler_params=pltpu.CompilerParams(
            collective_id=1, has_side_effects=True, vmem_limit_bytes=62 * 2**20
        ),
        name="newton_residual",
    )(
        candidate_rows, sigma_rows, sigma_sq_rows,
        direction.reshape(4, ROWS), relaxed.reshape(1, ROWS),
    )
    return result.reshape(ROWS)


def solution(mesh):
    return jax.shard_map(
        body,
        mesh=mesh,
        in_specs=(
            P("cand", "param"),
            P("cand", "param"),
            P("cand", "param"),
            P("cand"),
            P(("cand", "param")),
        ),
        out_specs=P(("cand", "param")),
        check_vma=False,
    )
```

```python
import jax
import jax.numpy as jnp
from jax import lax
from jax.experimental import pallas as pl
from jax.experimental.pallas import tpu as pltpu
from jax.sharding import PartitionSpec as P

PARTNERS = 2
barrier_weight = 0.1

MESH = pl.DeviceIdType.MESH
ROWS = 128
CHUNKS = 4
STEPS = 3 * CHUNKS
WHOLE = STEPS - 1
PIECE = 64
PIECES = 8
HALF = 256
SPAN = 256
AHEAD = 2
LAG = 4
REACH = 125.0
LAST = (((1,), (1,)), ((), ()))
FIRST = (((1,), (0,)), ((), ()))


def exact_dot(left, right, dims):
    return lax.dot_general(
        left, right, dims, precision=lax.Precision.HIGHEST, preferred_element_type=jnp.float32
    )


def coded(values):
    scale = jnp.max(jnp.abs(values), axis=0, keepdims=True) + 1e-30
    power = jnp.exp2(jnp.abs(values) * (2.0 * REACH / scale) - REACH)
    return jnp.where(values < 0.0, -power, power), scale


def decoded(code, scale):
    size = (jnp.log2(jnp.abs(code)) + REACH) * (scale * (0.5 / REACH))
    return jnp.where(code < 0.0, -size, size)


def kernel(
    a_in, s_in, q_in, v_in, z_in, out, own,
    rows, sq, sqt, own_vec, vec, g_send, g_recv, g_own, k_send, k_recv, w_send, w_recv, col, m_send, m_recv,
    load_sem, z_send_sem, z_recv_sem, x_send_sem, x_recv_sem, g_send_sem, g_recv_sem,
    k_send_sem, k_recv_sem, w_send_sem, w_recv_sem, m_send_sem, m_recv_sem, v_send_sem, v_recv_sem,
):
    cand, param = lax.axis_index("cand"), lax.axis_index("param")
    blocks = lax.axis_size("cand")
    odd, core, x_hi = lax.rem(cand, 2), lax.rem(param, 2), param // 2

    def block_at(by):
        return lax.rem(cand + blocks + by, blocks)

    loads = []
    for half in range(2):
        part = pl.ds(half * HALF, HALF)
        loads.append((s_in.at[part], sq.at[half, pl.ds(0, HALF)]))
        loads.append((q_in.at[part], sq.at[half, pl.ds(HALF, HALF)]))
    loads.append((a_in, rows.at[0]))
    loads = [
        pltpu.make_async_copy(source, target, load_sem.at[i])
        for i, (source, target) in enumerate(loads)
    ]
    for load in loads:
        load.start()

    barrier = pltpu.get_barrier_semaphore()
    partners = 0
    for by in (-2, -1, 0, 1, 2):
        for turn in range(4):
            if by == 0 and turn == 0:
                continue
            pl.semaphore_signal(
                barrier, inc=1, device_id=(block_at(by), lax.rem(param + turn, 4)),
                device_id_type=MESH,
            )
            partners += 1
    for part in range(4):
        own_vec[part] = jnp.broadcast_to(v_in[part : part + 1, :].astype(jnp.float32), (8, ROWS))
    col[...] = jnp.zeros_like(col)
    pl.semaphore_wait(barrier, partners)

    def own_piece(piece):
        return a_in.at[pl.ds(pl.multiple_of(piece * PIECE, PIECE), PIECE)]

    def landing(by, piece):
        return rows.at[by, pl.ds(pl.multiple_of(piece * PIECE, PIECE), PIECE)]

    def to_two_before(piece):
        return pltpu.make_async_remote_copy(
            src_ref=own_piece(piece), dst_ref=landing(2, piece),
            send_sem=z_send_sem.at[piece], recv_sem=z_recv_sem.at[piece],
            device_id=(block_at(-2), param), device_id_type=MESH,
        )

    def to_pair(piece, source):
        return pltpu.make_async_remote_copy(
            src_ref=source, dst_ref=landing(1, piece),
            send_sem=x_send_sem.at[piece], recv_sem=x_recv_sem.at[piece],
            device_id=(cand + 1 - 2 * odd, param), device_id_type=MESH,
        )

    def vec_to(by):
        return pltpu.make_async_remote_copy(
            src_ref=own_vec, dst_ref=vec.at[by - 1],
            send_sem=v_send_sem.at[by - 1], recv_sem=v_recv_sem.at[by - 1],
            device_id=(block_at(-by), param), device_id_type=MESH,
        )

    def send_own(piece):
        to_two_before(piece).start()

        @pl.when(odd == 1)
        def _():
            to_pair(piece, own_piece(piece)).start()

    def pass_on(piece):
        to_two_before(piece).wait_recv()

        @pl.when(odd == 0)
        def _():
            to_pair(piece, landing(2, piece)).start()

        @pl.when(piece + AHEAD < PIECES)
        def _():
            send_own(piece + AHEAD)

    send_own(0)
    for by in (1, 2):
        vec_to(by).start()

    for load in loads[:4]:
        load.wait()

    def turn(piece, carry):
        at = pl.ds(pl.multiple_of(piece * SPAN, SPAN), SPAN)
        for half in range(2):
            sqt[half, at, :] = sq[half, :, at].T
        return carry

    lax.fori_loop(0, sq.shape[2] // SPAN, turn, 0)
    loads[4].wait()

    def place(step):
        late = jnp.maximum(step - CHUNKS, 0)
        by = jnp.where(step < CHUNKS, 0, 2 - lax.rem(late, 2))
        return by, jnp.where(step < CHUNKS, step, late // 2)

    def lines(step, half):
        if half is None:
            return step, pl.ds(0, ROWS), step
        return WHOLE, pl.ds(half * PIECE, PIECE), WHOLE + half

    def to_core(step, half=None):
        slot, part, turn = lines(step, half)
        return pltpu.make_async_remote_copy(
            src_ref=g_send.at[slot, part], dst_ref=g_recv.at[slot, part],
            send_sem=g_send_sem.at[turn], recv_sem=g_recv_sem.at[turn],
            device_id=(cand, param + 1 - 2 * core), device_id_type=MESH,
        )

    def to_chip(step, half=None):
        slot, part, turn = lines(step, half)
        return pltpu.make_async_remote_copy(
            src_ref=k_send.at[slot, part], dst_ref=k_recv.at[slot, part],
            send_sem=k_send_sem.at[turn], recv_sem=k_recv_sem.at[turn],
            device_id=(cand, lax.rem(param + 2, 4)), device_id_type=MESH,
        )

    def scale_to_chip(step, half=None):
        turn = lines(step, half)[2]
        return pltpu.make_async_remote_copy(
            src_ref=w_send.at[turn], dst_ref=w_recv.at[turn],
            send_sem=w_send_sem.at[turn], recv_sem=w_recv_sem.at[turn],
            device_id=(cand, lax.rem(param + 2, 4)), device_id_type=MESH,
        )

    def message(index, slot, by, target):
        return pltpu.make_async_remote_copy(
            src_ref=m_send.at[index], dst_ref=m_recv.at[slot],
            send_sem=m_send_sem.at[index], recv_sem=m_recv_sem.at[slot],
            device_id=(block_at(by), target), device_id_type=MESH,
        )

    def products(step):
        by, chunk = place(step)

        for early in range(1, AHEAD):
            @pl.when(step == early)
            def _():
                send_own(early)

        @pl.when(step == CHUNKS)
        def _():
            pass_on(0)

        @pl.when(step >= CHUNKS)
        def _():
            pass_on(step - CHUNKS + 1)

        @pl.when(by == 1)
        def _():
            for part in range(2):
                to_pair(2 * chunk + part, landing(2, 2 * chunk + part)).wait_recv()

        multiply(rows[by, pl.ds(pl.multiple_of(chunk * ROWS, ROWS), ROWS), :], step, None)

    def last_products(half):
        piece = PIECES - 2 + half
        to_pair(piece, landing(2, piece)).wait_recv()
        multiply(rows[1, piece * PIECE : (piece + 1) * PIECE, :], WHOLE, half)

    def multiply(left, step, half):
        slot, part, _ = lines(step, half)
        g_send[slot, part] = lax.dot_general(
            left, sqt[1 - core], FIRST, preferred_element_type=jnp.float32
        )
        to_core(step, half).start()
        g_own[slot, part] = lax.dot_general(
            left, sqt[core], FIRST, preferred_element_type=jnp.float32
        )

    def between_cores(step, half=None):
        slot, part, turn = lines(step, half)
        to_core(step, half).wait_recv()
        total = g_own[slot, part] + g_recv[slot, part]
        g_own[slot, part] = total
        code, scale = coded(total[:, HALF:])
        k_send[slot, part] = code.astype(jnp.bfloat16)
        w_send[turn] = scale
        to_chip(step, half).start()
        scale_to_chip(step, half).start()

    def between_chips(step, halves=(None,)):
        by, chunk = place(step)
        other = []
        for half in halves:
            slot, part, turn = lines(step, half)
            to_chip(step, half).wait_recv()
            scale_to_chip(step, half).wait_recv()
            other.append(decoded(k_recv[slot, part].astype(jnp.float32), w_recv[turn]))
        other = jnp.concatenate(other, axis=0) if len(other) > 1 else other[0]
        total = g_own[step]
        tile = total[:, :HALF] * (total[:, HALF:] + other)
        half_vec = jnp.concatenate([own_vec[2 * core], own_vec[2 * core + 1]], axis=1)
        m_send[step] = exact_dot(2.0 * half_vec, tile, LAST)
        stays = jnp.logical_and(by == 0, chunk == param)

        @pl.when(stays)
        def _():
            m_recv[param] = m_send[step]

        @pl.when(jnp.logical_not(stays))
        def _():
            message(step, by * 4 + param, by, chunk).start()

        @pl.when(by > 0)
        def _():
            col[...] += exact_dot(2.0 * vec[jnp.maximum(by - 1, 0), chunk], tile, FIRST)

        @pl.when(jnp.logical_and(by == 0, chunk // 2 == core))
        def _():
            down = lax.broadcasted_iota(jnp.int32, (ROWS, HALF), 0)
            across = lax.broadcasted_iota(jnp.int32, (ROWS, HALF), 1)
            square = jnp.where(down + lax.rem(chunk, 2) * ROWS == across, total[:, HALF:], 0.0)
            col[...] -= jnp.broadcast_to(jnp.sum(square, axis=0, keepdims=True), (8, HALF))

    def first(step, carry):
        products(step)

        @pl.when(step >= 1)
        def _():
            between_cores(step - 1)

        return carry

    wait = jnp.where(odd == 0, 3, 1)

    def later(step, carry):
        products(step)

        @pl.when(step >= LAG)
        def _():
            between_chips(step - LAG)

        @pl.when(step >= CHUNKS + wait)
        def _():
            between_cores(step - wait)

        return carry

    def left_over(step, carry):
        between_cores(step)
        return carry

    def last(step, carry):
        between_chips(step)
        return carry

    lax.fori_loop(0, CHUNKS, first, 0)
    between_cores(CHUNKS - 1)
    for by in (1, 2):
        vec_to(by).wait()
    lax.fori_loop(CHUNKS, WHOLE, later, 0)
    lax.fori_loop(WHOLE - wait, WHOLE - 1, left_over, 0)
    last_products(0)
    between_chips(WHOLE - LAG)
    between_cores(WHOLE - 1)
    between_cores(WHOLE, 0)
    last_products(1)
    between_chips(WHOLE - LAG + 1)
    between_cores(WHOLE, 1)
    lax.fori_loop(WHOLE - LAG + 2, WHOLE, last, 0)

    zval = z_in[...]
    slope = barrier_weight * (1.0 / zval - 1.0 / (1.0 - zval))
    curve = barrier_weight * (1.0 / (zval * zval) + 1.0 / ((1.0 - zval) * (1.0 - zval)))
    own[...] = curve * own_vec[param][:1] - slope

    def drain(step, carry):
        to_core(step).wait_send()
        to_chip(step).wait_send()
        scale_to_chip(step).wait_send()
        return carry

    lax.fori_loop(0, WHOLE, drain, 0)
    for piece in range(PIECES):
        to_two_before(piece).wait_send()
        to_pair(piece, landing(2, piece)).wait_send()

    between_chips(WHOLE, (0, 1))

    for part in range(2):
        m_send[STEPS + part] = col[:, part * ROWS : (part + 1) * ROWS]
        target = 2 * core + part

        @pl.when(target == param)
        def _():
            m_recv[12 + x_hi] = m_send[STEPS + part]

        @pl.when(target != param)
        def _():
            message(STEPS + part, 12 + x_hi, 0, target).start()

    for half in range(2):
        to_core(WHOLE, half).wait_send()
        to_chip(WHOLE, half).wait_send()
        scale_to_chip(WHOLE, half).wait_send()

    def sent(step, carry):
        by, chunk = place(step)

        @pl.when(jnp.logical_not(jnp.logical_and(by == 0, chunk == param)))
        def _():
            message(step, 0, by, chunk).wait_send()

        return carry

    lax.fori_loop(0, STEPS, sent, 0)
    for part in range(2):
        @pl.when(2 * core + part != param)
        def _():
            message(STEPS + part, 0, 0, param).wait_send()

    for source in range(4):
        @pl.when(source != param)
        def _():
            message(0, source, 0, param).wait_recv()

        message(0, 4 + source, 1, param).wait_recv()
        message(0, 8 + source, 2, param).wait_recv()
    for high in range(2):
        @pl.when(2 * high + param // 2 != param)
        def _():
            message(0, 12 + high, 0, param).wait_recv()

    out[...] = jnp.sum(m_recv[...], axis=0)[:1]


def body(candidate_rows, sigma_rows, sigma_sq_rows, direction, relaxed):
    width, depth = candidate_rows.shape
    f32, bf16 = jnp.float32, jnp.bfloat16
    dma = pltpu.SemaphoreType.DMA
    product, own_terms = pl.pallas_call(
        kernel,
        out_shape=[jax.ShapeDtypeStruct((1, ROWS), f32)] * 2,
        in_specs=[pl.BlockSpec(memory_space=pl.ANY)] * 3
        + [pl.BlockSpec(memory_space=pltpu.VMEM)] * 2,
        out_specs=[pl.BlockSpec(memory_space=pltpu.VMEM)] * 2,
        scratch_shapes=[
            pltpu.VMEM((3, width, depth), bf16),
            pltpu.VMEM((2, width, depth), bf16),
            pltpu.VMEM((2, depth, width), bf16),
            pltpu.VMEM((4, 8, ROWS), f32),
            pltpu.VMEM((2, 4, 8, ROWS), f32),
            pltpu.VMEM((STEPS, ROWS, width), f32),
            pltpu.VMEM((STEPS, ROWS, width), f32),
            pltpu.VMEM((STEPS, ROWS, width), f32),
            pltpu.VMEM((STEPS, ROWS, HALF), bf16),
            pltpu.VMEM((STEPS, ROWS, HALF), bf16),
            pltpu.VMEM((STEPS + 1, 1, HALF), f32),
            pltpu.VMEM((STEPS + 1, 1, HALF), f32),
            pltpu.VMEM((8, HALF), f32),
            pltpu.VMEM((STEPS + 2, 8, ROWS), f32),
            pltpu.VMEM((14, 8, ROWS), f32),
            dma((5,)),
            dma((PIECES,)), dma((PIECES,)), dma((PIECES,)), dma((PIECES,)),
            dma((STEPS + 1,)), dma((STEPS + 1,)), dma((STEPS + 1,)),
            dma((STEPS + 1,)), dma((STEPS + 1,)), dma((STEPS + 1,)),
            dma((STEPS + 2,)), dma((14,)), dma((2,)), dma((2,)),
        ],
        compiler_params=pltpu.CompilerParams(
            collective_id=1, has_side_effects=True, vmem_limit_bytes=62 * 2**20
        ),
        name="newton_residual",
    )(
        candidate_rows, sigma_rows, sigma_sq_rows,
        direction.reshape(4, ROWS), relaxed.reshape(1, ROWS),
    )
    return (product + own_terms).reshape(ROWS)


def solution(mesh):
    return jax.shard_map(
        body,
        mesh=mesh,
        in_specs=(
            P("cand", "param"),
            P("cand", "param"),
            P("cand", "param"),
            P("cand"),
            P(("cand", "param")),
        ),
        out_specs=P(("cand", "param")),
        check_vma=False,
    )
```

```python
import jax
import jax.numpy as jnp
from jax import lax
from jax.experimental import pallas as pl
from jax.experimental.pallas import tpu as pltpu
from jax.sharding import PartitionSpec as P

PARTNERS = 2
barrier_weight = 0.1

MESH = pl.DeviceIdType.MESH
ROWS = 128
CHUNKS = 4
STEPS = 3 * CHUNKS
WHOLE = STEPS - 1
PIECE = 64
PIECES = 8
HALF = 256
SPAN = 256
AHEAD = 2
DETOUR = range(7, 9)
LAG = 5
REACH = 125.0
LAST = (((1,), (1,)), ((), ()))
FIRST = (((1,), (0,)), ((), ()))


def exact_dot(left, right, dims):
    return lax.dot_general(
        left, right, dims, precision=lax.Precision.HIGHEST, preferred_element_type=jnp.float32
    )


def coded(values):
    scale = jnp.max(jnp.abs(values), axis=0, keepdims=True) + 1e-30
    power = jnp.exp2(jnp.abs(values) * (2.0 * REACH / scale) - REACH)
    return jnp.where(values < 0.0, -power, power), scale


def decoded(code, scale):
    size = (jnp.log2(jnp.abs(code)) + REACH) * (scale * (0.5 / REACH))
    return jnp.where(code < 0.0, -size, size)


def kernel(
    a_in, s_in, q_in, v_in, z_in, out, own,
    rows, sq, sqt, own_vec, vec, g_send, g_recv, g_own, k_send, k_recv, w_send, w_recv, relay, col, m_send, m_recv,
    load_sem, z_send_sem, z_recv_sem, x_send_sem, x_recv_sem, g_send_sem, g_recv_sem,
    k_send_sem, k_recv_sem, w_send_sem, w_recv_sem, r_send_sem, r_recv_sem, m_send_sem, m_recv_sem, v_send_sem, v_recv_sem,
):
    cand, param = lax.axis_index("cand"), lax.axis_index("param")
    blocks = lax.axis_size("cand")
    odd, core, x_hi = lax.rem(cand, 2), lax.rem(param, 2), param // 2

    def block_at(by):
        return lax.rem(cand + blocks + by, blocks)

    loads = []
    for half in range(2):
        part = pl.ds(half * HALF, HALF)
        loads.append((s_in.at[part], sq.at[half, pl.ds(0, HALF)]))
        loads.append((q_in.at[part], sq.at[half, pl.ds(HALF, HALF)]))
    loads.append((a_in, rows.at[0]))
    loads = [
        pltpu.make_async_copy(source, target, load_sem.at[i])
        for i, (source, target) in enumerate(loads)
    ]
    for load in loads:
        load.start()

    barrier = pltpu.get_barrier_semaphore()
    partners = 0
    for by in (-2, -1, 0, 1, 2):
        for turn in range(4):
            if by == 0 and turn == 0:
                continue
            pl.semaphore_signal(
                barrier, inc=1, device_id=(block_at(by), lax.rem(param + turn, 4)),
                device_id_type=MESH,
            )
            partners += 1
    for part in range(4):
        own_vec[part] = jnp.broadcast_to(v_in[part : part + 1, :].astype(jnp.float32), (8, ROWS))
    col[...] = jnp.zeros_like(col)
    pl.semaphore_wait(barrier, partners)

    def own_piece(piece):
        return a_in.at[pl.ds(pl.multiple_of(piece * PIECE, PIECE), PIECE)]

    def landing(by, piece):
        return rows.at[by, pl.ds(pl.multiple_of(piece * PIECE, PIECE), PIECE)]

    def to_two_before(piece):
        return pltpu.make_async_remote_copy(
            src_ref=own_piece(piece), dst_ref=landing(2, piece),
            send_sem=z_send_sem.at[piece], recv_sem=z_recv_sem.at[piece],
            device_id=(block_at(-2), param), device_id_type=MESH,
        )

    def to_pair(piece, source):
        return pltpu.make_async_remote_copy(
            src_ref=source, dst_ref=landing(1, piece),
            send_sem=x_send_sem.at[piece], recv_sem=x_recv_sem.at[piece],
            device_id=(cand + 1 - 2 * odd, param), device_id_type=MESH,
        )

    def vec_to(by):
        return pltpu.make_async_remote_copy(
            src_ref=own_vec, dst_ref=vec.at[by - 1],
            send_sem=v_send_sem.at[by - 1], recv_sem=v_recv_sem.at[by - 1],
            device_id=(block_at(-by), param), device_id_type=MESH,
        )

    def send_own(piece):
        to_two_before(piece).start()

        @pl.when(odd == 1)
        def _():
            to_pair(piece, own_piece(piece)).start()

    def pass_on(piece):
        to_two_before(piece).wait_recv()

        @pl.when(odd == 0)
        def _():
            to_pair(piece, landing(2, piece)).start()

        @pl.when(piece + AHEAD < PIECES)
        def _():
            send_own(piece + AHEAD)

    send_own(0)
    for by in (1, 2):
        vec_to(by).start()

    for load in loads[:4]:
        load.wait()

    def turn(piece, carry):
        at = pl.ds(pl.multiple_of(piece * SPAN, SPAN), SPAN)
        for half in range(2):
            sqt[half, at, :] = sq[half, :, at].T
        return carry

    lax.fori_loop(0, sq.shape[2] // SPAN, turn, 0)
    loads[4].wait()

    def place(step):
        late = jnp.maximum(step - CHUNKS, 0)
        by = jnp.where(step < CHUNKS, 0, 2 - lax.rem(late, 2))
        return by, jnp.where(step < CHUNKS, step, late // 2)

    def lines(step, half):
        if half is None:
            return step, pl.ds(0, ROWS), step
        return WHOLE, pl.ds(half * PIECE, PIECE), WHOLE + half

    def to_core(step, half=None):
        slot, part, turn = lines(step, half)
        return pltpu.make_async_remote_copy(
            src_ref=g_send.at[slot, part], dst_ref=g_recv.at[slot, part],
            send_sem=g_send_sem.at[turn], recv_sem=g_recv_sem.at[turn],
            device_id=(cand, param + 1 - 2 * core), device_id_type=MESH,
        )

    def to_chip(step, half=None):
        slot, part, turn = lines(step, half)
        return pltpu.make_async_remote_copy(
            src_ref=k_send.at[slot, part], dst_ref=k_recv.at[slot, part],
            send_sem=k_send_sem.at[turn], recv_sem=k_recv_sem.at[turn],
            device_id=(cand, lax.rem(param + 2, 4)), device_id_type=MESH,
        )

    def by_odd(step):
        inside = jnp.logical_and(step >= DETOUR.start, step < DETOUR.stop)
        return jnp.logical_and(odd == 0, inside)

    def to_relay(step):
        index = step - DETOUR.start
        return pltpu.make_async_remote_copy(
            src_ref=k_send.at[step], dst_ref=relay.at[index],
            send_sem=k_send_sem.at[step], recv_sem=r_recv_sem.at[index],
            device_id=(block_at(1), lax.rem(param + 2, 4)), device_id_type=MESH,
        )

    def from_relay(step):
        index = step - DETOUR.start
        return pltpu.make_async_remote_copy(
            src_ref=relay.at[index], dst_ref=k_recv.at[step],
            send_sem=r_send_sem.at[index], recv_sem=k_recv_sem.at[step],
            device_id=(block_at(-1), param), device_id_type=MESH,
        )

    def hand_back(step):
        inside = jnp.logical_and(step >= DETOUR.start, step < DETOUR.stop)

        @pl.when(jnp.logical_and(odd == 1, inside))
        def _():
            to_relay(step).wait_recv()
            from_relay(step).start()

    def scale_to_chip(step, half=None):
        turn = lines(step, half)[2]
        return pltpu.make_async_remote_copy(
            src_ref=w_send.at[turn], dst_ref=w_recv.at[turn],
            send_sem=w_send_sem.at[turn], recv_sem=w_recv_sem.at[turn],
            device_id=(cand, lax.rem(param + 2, 4)), device_id_type=MESH,
        )

    def message(index, slot, by, target):
        return pltpu.make_async_remote_copy(
            src_ref=m_send.at[index], dst_ref=m_recv.at[slot],
            send_sem=m_send_sem.at[index], recv_sem=m_recv_sem.at[slot],
            device_id=(block_at(by), target), device_id_type=MESH,
        )

    def products(step):
        by, chunk = place(step)

        for early in range(1, AHEAD):
            @pl.when(step == early)
            def _():
                send_own(early)

        @pl.when(step == CHUNKS)
        def _():
            pass_on(0)

        @pl.when(step >= CHUNKS)
        def _():
            pass_on(step - CHUNKS + 1)

        @pl.when(by == 1)
        def _():
            for part in range(2):
                to_pair(2 * chunk + part, landing(2, 2 * chunk + part)).wait_recv()

        multiply(rows[by, pl.ds(pl.multiple_of(chunk * ROWS, ROWS), ROWS), :], step, None)

    def last_products(half):
        piece = PIECES - 2 + half
        to_pair(piece, landing(2, piece)).wait_recv()
        multiply(rows[1, piece * PIECE : (piece + 1) * PIECE, :], WHOLE, half)

    def multiply(left, step, half):
        slot, part, _ = lines(step, half)
        g_send[slot, part] = lax.dot_general(
            left, sqt[1 - core], FIRST, preferred_element_type=jnp.float32
        )
        to_core(step, half).start()
        g_own[slot, part] = lax.dot_general(
            left, sqt[core], FIRST, preferred_element_type=jnp.float32
        )

    def between_cores(step, half=None):
        slot, part, turn = lines(step, half)
        to_core(step, half).wait_recv()
        total = g_own[slot, part] + g_recv[slot, part]
        g_own[slot, part] = total
        code, scale = coded(total[:, HALF:])
        k_send[slot, part] = code.astype(jnp.bfloat16)
        w_send[turn] = scale
        if half is None:
            @pl.when(by_odd(step))
            def _():
                to_relay(step).start()

            @pl.when(jnp.logical_not(by_odd(step)))
            def _():
                to_chip(step).start()
        else:
            to_chip(step, half).start()
        scale_to_chip(step, half).start()

    def between_chips(step, halves=(None,)):
        by, chunk = place(step)
        other = []
        for half in halves:
            slot, part, turn = lines(step, half)
            to_chip(step, half).wait_recv()
            scale_to_chip(step, half).wait_recv()
            other.append(decoded(k_recv[slot, part].astype(jnp.float32), w_recv[turn]))
        other = jnp.concatenate(other, axis=0) if len(other) > 1 else other[0]
        total = g_own[step]
        tile = total[:, :HALF] * (total[:, HALF:] + other)
        half_vec = jnp.concatenate([own_vec[2 * core], own_vec[2 * core + 1]], axis=1)
        m_send[step] = exact_dot(2.0 * half_vec, tile, LAST)
        stays = jnp.logical_and(by == 0, chunk == param)

        @pl.when(stays)
        def _():
            m_recv[param] = m_send[step]

        @pl.when(jnp.logical_not(stays))
        def _():
            message(step, by * 4 + param, by, chunk).start()

        @pl.when(by > 0)
        def _():
            col[...] += exact_dot(2.0 * vec[jnp.maximum(by - 1, 0), chunk], tile, FIRST)

        @pl.when(jnp.logical_and(by == 0, chunk // 2 == core))
        def _():
            down = lax.broadcasted_iota(jnp.int32, (ROWS, HALF), 0)
            across = lax.broadcasted_iota(jnp.int32, (ROWS, HALF), 1)
            square = jnp.where(down + lax.rem(chunk, 2) * ROWS == across, total[:, HALF:], 0.0)
            col[...] -= jnp.broadcast_to(jnp.sum(square, axis=0, keepdims=True), (8, HALF))

    def first(step, carry):
        products(step)

        @pl.when(step >= 1)
        def _():
            between_cores(step - 1)

        return carry

    wait = jnp.where(odd == 0, 1, 1)

    def later(step, carry):
        hand_back(step - 2)
        products(step)

        @pl.when(step >= LAG)
        def _():
            between_chips(step - LAG)

        @pl.when(step >= CHUNKS + wait)
        def _():
            between_cores(step - wait)

        return carry

    def left_over(step, carry):
        between_cores(step)
        return carry

    def last(step, carry):
        between_chips(step)
        return carry

    lax.fori_loop(0, CHUNKS, first, 0)
    between_cores(CHUNKS - 1)
    for by in (1, 2):
        vec_to(by).wait()
    lax.fori_loop(CHUNKS, WHOLE, later, 0)
    lax.fori_loop(WHOLE - wait, WHOLE - 1, left_over, 0)
    last_products(0)
    between_chips(WHOLE - LAG)
    between_cores(WHOLE - 1)
    between_cores(WHOLE, 0)
    last_products(1)
    between_chips(WHOLE - LAG + 1)
    between_cores(WHOLE, 1)
    lax.fori_loop(WHOLE - LAG + 2, WHOLE, last, 0)

    zval = z_in[...]
    slope = barrier_weight * (1.0 / zval - 1.0 / (1.0 - zval))
    curve = barrier_weight * (1.0 / (zval * zval) + 1.0 / ((1.0 - zval) * (1.0 - zval)))
    own[...] = curve * own_vec[param][:1] - slope

    def drain(step, carry):
        to_core(step).wait_send()
        to_chip(step).wait_send()
        scale_to_chip(step).wait_send()
        return carry

    lax.fori_loop(0, WHOLE, drain, 0)

    @pl.when(odd == 1)
    def _():
        for step in DETOUR:
            from_relay(step).wait_send()

    for piece in range(PIECES):
        to_two_before(piece).wait_send()
        to_pair(piece, landing(2, piece)).wait_send()

    between_chips(WHOLE, (0, 1))

    for part in range(2):
        m_send[STEPS + part] = col[:, part * ROWS : (part + 1) * ROWS]
        target = 2 * core + part

        @pl.when(target == param)
        def _():
            m_recv[12 + x_hi] = m_send[STEPS + part]

        @pl.when(target != param)
        def _():
            message(STEPS + part, 12 + x_hi, 0, target).start()

    for half in range(2):
        to_core(WHOLE, half).wait_send()
        to_chip(WHOLE, half).wait_send()
        scale_to_chip(WHOLE, half).wait_send()

    def sent(step, carry):
        by, chunk = place(step)

        @pl.when(jnp.logical_not(jnp.logical_and(by == 0, chunk == param)))
        def _():
            message(step, 0, by, chunk).wait_send()

        return carry

    lax.fori_loop(0, STEPS, sent, 0)
    for part in range(2):
        @pl.when(2 * core + part != param)
        def _():
            message(STEPS + part, 0, 0, param).wait_send()

    for source in range(4):
        @pl.when(source != param)
        def _():
            message(0, source, 0, param).wait_recv()

        message(0, 4 + source, 1, param).wait_recv()
        message(0, 8 + source, 2, param).wait_recv()
    for high in range(2):
        @pl.when(2 * high + param // 2 != param)
        def _():
            message(0, 12 + high, 0, param).wait_recv()

    out[...] = jnp.sum(m_recv[...], axis=0)[:1]


def body(candidate_rows, sigma_rows, sigma_sq_rows, direction, relaxed):
    width, depth = candidate_rows.shape
    f32, bf16 = jnp.float32, jnp.bfloat16
    dma = pltpu.SemaphoreType.DMA
    product, own_terms = pl.pallas_call(
        kernel,
        out_shape=[jax.ShapeDtypeStruct((1, ROWS), f32)] * 2,
        in_specs=[pl.BlockSpec(memory_space=pl.ANY)] * 3
        + [pl.BlockSpec(memory_space=pltpu.VMEM)] * 2,
        out_specs=[pl.BlockSpec(memory_space=pltpu.VMEM)] * 2,
        scratch_shapes=[
            pltpu.VMEM((3, width, depth), bf16),
            pltpu.VMEM((2, width, depth), bf16),
            pltpu.VMEM((2, depth, width), bf16),
            pltpu.VMEM((4, 8, ROWS), f32),
            pltpu.VMEM((2, 4, 8, ROWS), f32),
            pltpu.VMEM((STEPS, ROWS, width), f32),
            pltpu.VMEM((STEPS, ROWS, width), f32),
            pltpu.VMEM((STEPS, ROWS, width), f32),
            pltpu.VMEM((STEPS, ROWS, HALF), bf16),
            pltpu.VMEM((STEPS, ROWS, HALF), bf16),
            pltpu.VMEM((STEPS + 1, 1, HALF), f32),
            pltpu.VMEM((STEPS + 1, 1, HALF), f32),
            pltpu.VMEM((len(DETOUR), ROWS, HALF), bf16),
            pltpu.VMEM((8, HALF), f32),
            pltpu.VMEM((STEPS + 2, 8, ROWS), f32),
            pltpu.VMEM((14, 8, ROWS), f32),
            dma((5,)),
            dma((PIECES,)), dma((PIECES,)), dma((PIECES,)), dma((PIECES,)),
            dma((STEPS + 1,)), dma((STEPS + 1,)), dma((STEPS + 1,)),
            dma((STEPS + 1,)), dma((STEPS + 1,)), dma((STEPS + 1,)),
            dma((len(DETOUR),)), dma((len(DETOUR),)),
            dma((STEPS + 2,)), dma((14,)), dma((2,)), dma((2,)),
        ],
        compiler_params=pltpu.CompilerParams(
            collective_id=1, has_side_effects=True, vmem_limit_bytes=62 * 2**20
        ),
        name="newton_residual",
    )(
        candidate_rows, sigma_rows, sigma_sq_rows,
        direction.reshape(4, ROWS), relaxed.reshape(1, ROWS),
    )
    return (product + own_terms).reshape(ROWS)


def solution(mesh):
    return jax.shard_map(
        body,
        mesh=mesh,
        in_specs=(
            P("cand", "param"),
            P("cand", "param"),
            P("cand", "param"),
            P("cand"),
            P(("cand", "param")),
        ),
        out_specs=P(("cand", "param")),
        check_vma=False,
    )
```

```python
import jax
import jax.numpy as jnp
from jax import lax
from jax.experimental import pallas as pl
from jax.experimental.pallas import tpu as pltpu
from jax.sharding import PartitionSpec as P

PARTNERS = 2
barrier_weight = 0.1

MESH = pl.DeviceIdType.MESH
ROWS = 128
CHUNKS = 4
STEPS = 3 * CHUNKS
WHOLE = STEPS - 1
PIECE = 64
PIECES = 8
HALF = 256
SPAN = 256
AHEAD = 2
DETOUR = range(7, 9)
LAG = 5
REACH = 125.0
LAST = (((1,), (1,)), ((), ()))
FIRST = (((1,), (0,)), ((), ()))


def exact_dot(left, right, dims):
    return lax.dot_general(
        left, right, dims, precision=lax.Precision.HIGHEST, preferred_element_type=jnp.float32
    )


def coded(values):
    scale = jnp.max(jnp.abs(values), axis=0, keepdims=True) + 1e-30
    power = jnp.exp2(jnp.abs(values) * (2.0 * REACH / scale) - REACH)
    return jnp.where(values < 0.0, -power, power), scale


def decoded(code, scale):
    size = (jnp.log2(jnp.abs(code)) + REACH) * (scale * (0.5 / REACH))
    return jnp.where(code < 0.0, -size, size)


def kernel(
    a_in, s_in, q_in, v_in, z_in, out, own,
    rows, sq, sqt, own_vec, vec, g_send, g_recv, g_own, k_send, k_recv, w_send, w_recv, relay, col, m_send, m_recv,
    load_sem, z_send_sem, z_recv_sem, x_send_sem, x_recv_sem, g_send_sem, g_recv_sem,
    k_send_sem, k_recv_sem, w_send_sem, w_recv_sem, r_send_sem, r_recv_sem, m_send_sem, m_recv_sem, v_send_sem, v_recv_sem,
):
    cand, param = lax.axis_index("cand"), lax.axis_index("param")
    blocks = lax.axis_size("cand")
    odd, core, x_hi = lax.rem(cand, 2), lax.rem(param, 2), param // 2

    def block_at(by):
        return lax.rem(cand + blocks + by, blocks)

    loads = []
    for half in range(2):
        part = pl.ds(half * HALF, HALF)
        loads.append((s_in.at[part], sq.at[half, pl.ds(0, HALF)]))
        loads.append((q_in.at[part], sq.at[half, pl.ds(HALF, HALF)]))
    loads.append((a_in, rows.at[0]))
    loads = [
        pltpu.make_async_copy(source, target, load_sem.at[i])
        for i, (source, target) in enumerate(loads)
    ]
    for load in loads:
        load.start()

    barrier = pltpu.get_barrier_semaphore()
    partners = 0
    for by in (-2, -1, 0, 1, 2):
        for turn in range(4):
            if by == 0 and turn == 0:
                continue
            pl.semaphore_signal(
                barrier, inc=1, device_id=(block_at(by), lax.rem(param + turn, 4)),
                device_id_type=MESH,
            )
            partners += 1
    for part in range(4):
        own_vec[part] = jnp.broadcast_to(v_in[part : part + 1, :].astype(jnp.float32), (8, ROWS))
    col[...] = jnp.zeros_like(col)
    pl.semaphore_wait(barrier, partners)

    def own_piece(piece):
        return a_in.at[pl.ds(pl.multiple_of(piece * PIECE, PIECE), PIECE)]

    def landing(by, piece):
        return rows.at[by, pl.ds(pl.multiple_of(piece * PIECE, PIECE), PIECE)]

    def to_two_before(piece):
        return pltpu.make_async_remote_copy(
            src_ref=own_piece(piece), dst_ref=landing(2, piece),
            send_sem=z_send_sem.at[piece], recv_sem=z_recv_sem.at[piece],
            device_id=(block_at(-2), param), device_id_type=MESH,
        )

    def to_pair(piece, source):
        return pltpu.make_async_remote_copy(
            src_ref=source, dst_ref=landing(1, piece),
            send_sem=x_send_sem.at[piece], recv_sem=x_recv_sem.at[piece],
            device_id=(cand + 1 - 2 * odd, param), device_id_type=MESH,
        )

    def vec_to(by):
        return pltpu.make_async_remote_copy(
            src_ref=own_vec, dst_ref=vec.at[by - 1],
            send_sem=v_send_sem.at[by - 1], recv_sem=v_recv_sem.at[by - 1],
            device_id=(block_at(-by), param), device_id_type=MESH,
        )

    def send_own(piece):
        to_two_before(piece).start()

        @pl.when(odd == 1)
        def _():
            to_pair(piece, own_piece(piece)).start()

    def pass_on(piece):
        to_two_before(piece).wait_recv()

        @pl.when(odd == 0)
        def _():
            to_pair(piece, landing(2, piece)).start()

        @pl.when(piece + AHEAD < PIECES)
        def _():
            send_own(piece + AHEAD)

    send_own(0)
    for by in (1, 2):
        vec_to(by).start()

    for load in loads[:4]:
        load.wait()

    def turn(piece, carry):
        at = pl.ds(pl.multiple_of(piece * SPAN, SPAN), SPAN)
        for half in range(2):
            sqt[half, at, :] = sq[half, :, at].T
        return carry

    lax.fori_loop(0, sq.shape[2] // SPAN, turn, 0)
    loads[4].wait()

    def place(step):
        late = jnp.maximum(step - CHUNKS, 0)
        by = jnp.where(step < CHUNKS, 0, 2 - lax.rem(late, 2))
        return by, jnp.where(step < CHUNKS, step, late // 2)

    def lines(step, half):
        if half is None:
            return step, pl.ds(0, ROWS), step
        return WHOLE, pl.ds(half * PIECE, PIECE), WHOLE + half

    def to_core(step, half=None):
        slot, part, turn = lines(step, half)
        return pltpu.make_async_remote_copy(
            src_ref=g_send.at[slot, part], dst_ref=g_recv.at[slot, part],
            send_sem=g_send_sem.at[turn], recv_sem=g_recv_sem.at[turn],
            device_id=(cand, param + 1 - 2 * core), device_id_type=MESH,
        )

    def to_chip(step, half=None):
        slot, part, turn = lines(step, half)
        return pltpu.make_async_remote_copy(
            src_ref=k_send.at[slot, part], dst_ref=k_recv.at[slot, part],
            send_sem=k_send_sem.at[turn], recv_sem=k_recv_sem.at[turn],
            device_id=(cand, lax.rem(param + 2, 4)), device_id_type=MESH,
        )

    def by_odd(step):
        inside = jnp.logical_and(step >= DETOUR.start, step < DETOUR.stop)
        return jnp.logical_and(odd == 0, inside)

    def to_relay(step):
        index = step - DETOUR.start
        return pltpu.make_async_remote_copy(
            src_ref=k_send.at[step], dst_ref=relay.at[index],
            send_sem=k_send_sem.at[step], recv_sem=r_recv_sem.at[index],
            device_id=(block_at(1), lax.rem(param + 2, 4)), device_id_type=MESH,
        )

    def from_relay(step):
        index = step - DETOUR.start
        return pltpu.make_async_remote_copy(
            src_ref=relay.at[index], dst_ref=k_recv.at[step],
            send_sem=r_send_sem.at[index], recv_sem=k_recv_sem.at[step],
            device_id=(block_at(-1), param), device_id_type=MESH,
        )

    def hand_back(step):
        inside = jnp.logical_and(step >= DETOUR.start, step < DETOUR.stop)

        @pl.when(jnp.logical_and(odd == 1, inside))
        def _():
            to_relay(step).wait_recv()
            from_relay(step).start()

    def scale_to_chip(step, half=None):
        turn = lines(step, half)[2]
        return pltpu.make_async_remote_copy(
            src_ref=w_send.at[turn], dst_ref=w_recv.at[turn],
            send_sem=w_send_sem.at[turn], recv_sem=w_recv_sem.at[turn],
            device_id=(cand, lax.rem(param + 2, 4)), device_id_type=MESH,
        )

    def message(index, slot, by, target):
        return pltpu.make_async_remote_copy(
            src_ref=m_send.at[index], dst_ref=m_recv.at[slot],
            send_sem=m_send_sem.at[index], recv_sem=m_recv_sem.at[slot],
            device_id=(block_at(by), target), device_id_type=MESH,
        )

    def products(step):
        by, chunk = place(step)

        for early in range(1, AHEAD):
            @pl.when(step == early)
            def _():
                send_own(early)

        @pl.when(step == CHUNKS)
        def _():
            pass_on(0)

        @pl.when(step >= CHUNKS)
        def _():
            pass_on(step - CHUNKS + 1)

        @pl.when(by == 1)
        def _():
            for part in range(2):
                to_pair(2 * chunk + part, landing(2, 2 * chunk + part)).wait_recv()

        multiply(rows[by, pl.ds(pl.multiple_of(chunk * ROWS, ROWS), ROWS), :], step, None)

    def last_products(half):
        piece = PIECES - 2 + half
        to_pair(piece, landing(2, piece)).wait_recv()
        multiply(rows[1, piece * PIECE : (piece + 1) * PIECE, :], WHOLE, half)

    def multiply(left, step, half):
        slot, part, _ = lines(step, half)
        g_send[slot, part] = lax.dot_general(
            left, sqt[1 - core], FIRST, preferred_element_type=jnp.float32
        )
        to_core(step, half).start()
        g_own[slot, part] = lax.dot_general(
            left, sqt[core], FIRST, preferred_element_type=jnp.float32
        )

    def between_cores(step, half=None):
        slot, part, turn = lines(step, half)
        to_core(step, half).wait_recv()
        total = g_own[slot, part] + g_recv[slot, part]
        g_own[slot, part] = total
        code, scale = coded(total[:, HALF:])
        k_send[slot, part] = code.astype(jnp.bfloat16)
        w_send[turn] = scale
        if half is None:
            @pl.when(by_odd(step))
            def _():
                to_relay(step).start()

            @pl.when(jnp.logical_not(by_odd(step)))
            def _():
                to_chip(step).start()
        else:
            to_chip(step, half).start()
        scale_to_chip(step, half).start()

    def between_chips(step, halves=(None,)):
        by, chunk = place(step)
        other = []
        for half in halves:
            slot, part, turn = lines(step, half)
            to_chip(step, half).wait_recv()
            scale_to_chip(step, half).wait_recv()
            other.append(decoded(k_recv[slot, part].astype(jnp.float32), w_recv[turn]))
        other = jnp.concatenate(other, axis=0) if len(other) > 1 else other[0]
        total = g_own[step]
        tile = total[:, :HALF] * (total[:, HALF:] + other)
        half_vec = jnp.concatenate([own_vec[2 * core], own_vec[2 * core + 1]], axis=1)
        m_send[step] = exact_dot(2.0 * half_vec, tile, LAST)
        stays = jnp.logical_and(by == 0, chunk == param)

        @pl.when(stays)
        def _():
            m_recv[param] = m_send[step]

        @pl.when(jnp.logical_not(stays))
        def _():
            message(step, by * 4 + param, by, chunk).start()

        @pl.when(by > 0)
        def _():
            col[...] += exact_dot(2.0 * vec[jnp.maximum(by - 1, 0), chunk], tile, FIRST)

        @pl.when(jnp.logical_and(by == 0, chunk // 2 == core))
        def _():
            down = lax.broadcasted_iota(jnp.int32, (ROWS, HALF), 0)
            across = lax.broadcasted_iota(jnp.int32, (ROWS, HALF), 1)
            square = jnp.where(down + lax.rem(chunk, 2) * ROWS == across, total[:, HALF:], 0.0)
            col[...] -= jnp.broadcast_to(jnp.sum(square, axis=0, keepdims=True), (8, HALF))

    def first(step, carry):
        products(step)

        @pl.when(step >= 1)
        def _():
            between_cores(step - 1)

        return carry

    wait = jnp.where(odd == 0, 1, 1)

    def later(step, carry):
        hand_back(step - 2)
        products(step)

        @pl.when(step >= LAG)
        def _():
            between_chips(step - LAG)

        @pl.when(step >= CHUNKS + wait)
        def _():
            between_cores(step - wait)

        return carry

    def left_over(step, carry):
        between_cores(step)
        return carry

    def last(step, carry):
        between_chips(step)
        return carry

    lax.fori_loop(0, CHUNKS, first, 0)
    between_cores(CHUNKS - 1)
    for by in (1, 2):
        vec_to(by).wait()
    lax.fori_loop(CHUNKS, WHOLE, later, 0)
    lax.fori_loop(WHOLE - wait, WHOLE, left_over, 0)
    last_products(0)
    between_chips(WHOLE - LAG)
    between_cores(WHOLE, 0)
    last_products(1)
    between_chips(WHOLE - LAG + 1)
    between_cores(WHOLE, 1)
    lax.fori_loop(WHOLE - LAG + 2, WHOLE, last, 0)

    zval = z_in[...]
    slope = barrier_weight * (1.0 / zval - 1.0 / (1.0 - zval))
    curve = barrier_weight * (1.0 / (zval * zval) + 1.0 / ((1.0 - zval) * (1.0 - zval)))
    own[...] = curve * own_vec[param][:1] - slope

    def drain(step, carry):
        to_core(step).wait_send()
        to_chip(step).wait_send()
        scale_to_chip(step).wait_send()
        return carry

    lax.fori_loop(0, WHOLE, drain, 0)

    @pl.when(odd == 1)
    def _():
        for step in DETOUR:
            from_relay(step).wait_send()

    for piece in range(PIECES):
        to_two_before(piece).wait_send()
        to_pair(piece, landing(2, piece)).wait_send()

    between_chips(WHOLE, (0, 1))

    for part in range(2):
        m_send[STEPS + part] = col[:, part * ROWS : (part + 1) * ROWS]
        target = 2 * core + part

        @pl.when(target == param)
        def _():
            m_recv[12 + x_hi] = m_send[STEPS + part]

        @pl.when(target != param)
        def _():
            message(STEPS + part, 12 + x_hi, 0, target).start()

    for half in range(2):
        to_core(WHOLE, half).wait_send()
        to_chip(WHOLE, half).wait_send()
        scale_to_chip(WHOLE, half).wait_send()

    def sent(step, carry):
        by, chunk = place(step)

        @pl.when(jnp.logical_not(jnp.logical_and(by == 0, chunk == param)))
        def _():
            message(step, 0, by, chunk).wait_send()

        return carry

    lax.fori_loop(0, STEPS, sent, 0)
    for part in range(2):
        @pl.when(2 * core + part != param)
        def _():
            message(STEPS + part, 0, 0, param).wait_send()

    for source in range(4):
        @pl.when(source != param)
        def _():
            message(0, source, 0, param).wait_recv()

        message(0, 4 + source, 1, param).wait_recv()
        message(0, 8 + source, 2, param).wait_recv()
    for high in range(2):
        @pl.when(2 * high + param // 2 != param)
        def _():
            message(0, 12 + high, 0, param).wait_recv()

    out[...] = jnp.sum(m_recv[...], axis=0)[:1]


def body(candidate_rows, sigma_rows, sigma_sq_rows, direction, relaxed):
    width, depth = candidate_rows.shape
    f32, bf16 = jnp.float32, jnp.bfloat16
    dma = pltpu.SemaphoreType.DMA
    product, own_terms = pl.pallas_call(
        kernel,
        out_shape=[jax.ShapeDtypeStruct((1, ROWS), f32)] * 2,
        in_specs=[pl.BlockSpec(memory_space=pl.ANY)] * 3
        + [pl.BlockSpec(memory_space=pltpu.VMEM)] * 2,
        out_specs=[pl.BlockSpec(memory_space=pltpu.VMEM)] * 2,
        scratch_shapes=[
            pltpu.VMEM((3, width, depth), bf16),
            pltpu.VMEM((2, width, depth), bf16),
            pltpu.VMEM((2, depth, width), bf16),
            pltpu.VMEM((4, 8, ROWS), f32),
            pltpu.VMEM((2, 4, 8, ROWS), f32),
            pltpu.VMEM((STEPS, ROWS, width), f32),
            pltpu.VMEM((STEPS, ROWS, width), f32),
            pltpu.VMEM((STEPS, ROWS, width), f32),
            pltpu.VMEM((STEPS, ROWS, HALF), bf16),
            pltpu.VMEM((STEPS, ROWS, HALF), bf16),
            pltpu.VMEM((STEPS + 1, 1, HALF), f32),
            pltpu.VMEM((STEPS + 1, 1, HALF), f32),
            pltpu.VMEM((len(DETOUR), ROWS, HALF), bf16),
            pltpu.VMEM((8, HALF), f32),
            pltpu.VMEM((STEPS + 2, 8, ROWS), f32),
            pltpu.VMEM((14, 8, ROWS), f32),
            dma((5,)),
            dma((PIECES,)), dma((PIECES,)), dma((PIECES,)), dma((PIECES,)),
            dma((STEPS + 1,)), dma((STEPS + 1,)), dma((STEPS + 1,)),
            dma((STEPS + 1,)), dma((STEPS + 1,)), dma((STEPS + 1,)),
            dma((len(DETOUR),)), dma((len(DETOUR),)),
            dma((STEPS + 2,)), dma((14,)), dma((2,)), dma((2,)),
        ],
        compiler_params=pltpu.CompilerParams(
            collective_id=1, has_side_effects=True, vmem_limit_bytes=62 * 2**20
        ),
        name="newton_residual",
    )(
        candidate_rows, sigma_rows, sigma_sq_rows,
        direction.reshape(4, ROWS), relaxed.reshape(1, ROWS),
    )
    return (product + own_terms).reshape(ROWS)


def solution(mesh):
    return jax.shard_map(
        body,
        mesh=mesh,
        in_specs=(
            P("cand", "param"),
            P("cand", "param"),
            P("cand", "param"),
            P("cand"),
            P(("cand", "param")),
        ),
        out_specs=P(("cand", "param")),
        check_vma=False,
    )
```
